512 devices in a mesh: dp: 64 (over z, x_hi, core), ctx: 8 (over x_lo, y).
Axes of the slice: x: 4 (x_hi: 2, x_lo: 2; x = x_hi * 2 + x_lo), y: 4, z: 16, core: 2. Of those that a mesh axis runs over, the one named last changes fastest.
Arguments:
- queries: bfloat16 [64, 1024, 2048], P('dp', 'ctx'), may hold values from -14.5 to 14.5
- keys: bfloat16 [64, 1024, 128], P('dp', 'ctx'), may hold values from -6 to 6
- values: bfloat16 [64, 1024, 128], P('dp', 'ctx'), may hold values from -6 to 6
- grad_out: bfloat16 [64, 1024, 2048], P('dp', 'ctx'), may hold values from -6 to 6
- doc_lengths: int32 [64, 8], replicated, may hold values from 1 to 512, 1024 in all within a row
- switches: int32 [6, 64], replicated, may hold values from 0 to 1, as said below
Outputs:
- attended: bfloat16 [64, 1024, 2048], P('dp', 'ctx')
- grad_queries: bfloat16 [64, 1024, 2048], P('dp', 'ctx')
- grad_keys: bfloat16 [64, 1024, 128], P('dp', 'ctx')
- grad_values: bfloat16 [64, 1024, 128], P('dp', 'ctx')
The draws below stay inside these ranges and needn't reach their ends.
Inputs may be any that keep to these rules, and one draw needn't show every extreme that they name: `doc_lengths`: each row sums to 1024; its largest entry is exactly 512. switches[b, r] equals switches[b, r XOR 2**b].
All inputs are finite; a program needn't handle non-finite values.
Results may differ from the reference program's by a relative error of at most 0.022.
Values may be sent and summed in bfloat16 or wider, within the bound.
A program may use at most 64 MiB of HBM per device.

```python
import math
import jax
import jax.numpy as jnp
import numpy as np
from jax import lax

HEAD = 128
GROUP = 16
DOCS = 8
SEQS = 64
LENGTH = 1024
LOG_DP = 6


def shared_rows(key):
    normal_part = jax.random.truncated_normal(jax.random.fold_in(key, 11), -6.0, 6.0, (SEQS, LENGTH, HEAD), jnp.float32)
    base = normal_part
    return base


def draw_keys(key, part):
    base = shared_rows(key)
    return base.astype(jnp.bfloat16)


def draw_queries(key, part):
    key = jax.random.fold_in(key, 3)
    return jax.random.truncated_normal(key, -6.0, 6.0, (SEQS, LENGTH, GROUP * HEAD), jnp.float32).astype(jnp.bfloat16)


def draw_switches(key, part):
    key = jax.random.fold_in(key, 5)
    raw = jax.random.randint(key, (LOG_DP, SEQS), 0, 2, dtype=jnp.int32)
    anchor = jnp.arange(SEQS, dtype=jnp.int32)
    stacked = []
    for section_index in range(LOG_DP):
        lower = anchor - anchor // 2 ** section_index % 2 * 2 ** section_index
        stacked.append(raw[section_index][lower])
    return jnp.stack(stacked)


def shard_levels(stream_key, extent, cuts, least, high):
    gain = 1.0
    for axis_at, blocks in cuts:
        steps = jax.random.uniform(jax.random.fold_in(jax.random.fold_in(stream_key, 6), axis_at), (blocks,), jnp.float32, least / len(cuts), high / len(cuts))
        gain = gain * jnp.repeat(jnp.exp(steps), extent[axis_at] // blocks).reshape((-1,) + (1,) * (len(extent) - 1 - axis_at))
    return gain


def length_profile(number_of, total, bound, lean):
    weights = [(1 << 20) // math.isqrt(grade ** lean) + 1 for grade in range(2, number_of + 1)]
    spare, given = total - bound - (number_of - 1), [1] * (number_of - 1)
    while spare > 0:
        candidates = [i for i in range(number_of - 1) if given[i] < bound]
        pool, budget = sum([weights[i] for i in candidates]), spare
        for i in candidates:
            more = min(bound - given[i], max(1, budget * weights[i] // pool), spare)
            given[i] = given[i] + more
            spare = spare - more
    return np.array([bound] + given)


def uneven(rng, number_of, total, reach, skew):
    if number_of == 2:
        one = jax.random.randint(rng, (), max(1, total - reach), min(reach, total - 1) + 1)
        return jnp.stack([one, total - one])
    tallies = jnp.asarray(length_profile(number_of, total, reach, skew), jnp.int32)
    twos = (number_of - 1) // 2
    giver, receiver = tallies[1:1 + 2 * twos:2], tallies[2:2 + 2 * twos:2]
    slack = jnp.minimum(giver - 1, reach - receiver)
    moved = jax.random.randint(jax.random.fold_in(rng, 1), (twos,), 0, 1 << 20) % (slack + 1)
    tallies = tallies.at[1:1 + 2 * twos:2].set(giver - moved).at[2:2 + 2 * twos:2].set(receiver + moved)
    return tallies[jax.random.permutation(jax.random.fold_in(rng, 2), number_of)]


def scatter_about(own_key, dims, scale, reach, split=(), kind=jnp.bfloat16):
    entries = scale * jax.random.normal(own_key, dims, jnp.float32)
    if split:
        entries = entries * shard_levels(own_key, dims, split, -0.22, 0.18)
    return jnp.clip(entries, -reach, reach).astype(kind)


def setup_inputs(seed: int = 0) -> dict:
    streams_of = jax.random.split(jax.random.key(seed), 7)
    queries = draw_queries(jax.random.fold_in(streams_of[6], 71), 0)
    keys = draw_keys(jax.random.fold_in(streams_of[6], 71), 0)
    values = scatter_about(streams_of[2], (SEQS, LENGTH, HEAD), 1.0, 6.0, ((0, 64), (1, 8)))
    grad_out = scatter_about(streams_of[3], (SEQS, LENGTH, GROUP * HEAD), 1.0, 6.0, ((0, 64), (1, 8)))
    doc_lengths = jax.vmap(lambda own: uneven(own, DOCS, LENGTH, LENGTH // 2, 2))(jax.random.split(streams_of[4], SEQS)).reshape((SEQS, DOCS)).astype(jnp.int32)
    switches = draw_switches(jax.random.fold_in(streams_of[6], 71), 0)
    return dict(queries=queries, keys=keys, values=values, grad_out=grad_out, doc_lengths=doc_lengths, switches=switches)


NEG_FILL = -1e30


def source_index(switches):
    seq_count = switches.shape[1]
    anchor = jnp.arange(seq_count, dtype=jnp.int32)
    where_from = anchor
    for section_index in range(switches.shape[0]):
        partner = jnp.bitwise_xor(anchor, jnp.int32(1 << section_index)).astype(jnp.int32)
        where_from = jnp.where(switches[section_index] == 1, where_from[partner], where_from)
    return where_from


def row_starts(lengths, positions):
    ends = jnp.cumsum(lengths).astype(jnp.int32)
    starts = (ends - lengths).astype(jnp.int32)
    chosen = jnp.where(starts[None, :] <= positions[:, None], starts[None, :], 0)
    return jnp.max(chosen, axis=1).astype(jnp.int32)


def one_sequence(inputs):
    queries, keys, values, grad_out, lengths = inputs
    length = queries.shape[0]
    head_size = keys.shape[1]
    score_scale = head_size ** -0.5
    positions = jnp.arange(length, dtype=jnp.int32)
    starts = row_starts(lengths, positions)
    allowed = (positions[None, :] <= positions[:, None]) & (positions[None, :] >= starts[:, None])
    query_heads = queries.reshape(length, -1, head_size).transpose(1, 0, 2)
    grad_heads = grad_out.reshape(length, -1, head_size).transpose(1, 0, 2)

    def one_head(pair):
        query_rows, grad_rows = pair
        scores = jnp.where(allowed, jnp.dot(query_rows, keys.T, preferred_element_type=jnp.float32) * score_scale, NEG_FILL)
        row_max = jnp.max(scores, axis=1, keepdims=True)
        row_sum = jnp.sum(jnp.where(allowed, jnp.exp(scores - row_max), 0.0), axis=1, keepdims=True)
        log_total = row_max + jnp.log(row_sum)
        weights = jnp.where(allowed, jnp.exp(scores - log_total), 0.0)
        rounded = weights.astype(jnp.bfloat16)
        attended = jnp.dot(rounded, values, preferred_element_type=jnp.float32).astype(jnp.bfloat16)
        row_dots = jnp.sum(attended.astype(jnp.float32) * grad_rows.astype(jnp.float32), axis=1, keepdims=True)
        grad_probs = jnp.dot(grad_rows, values.T, preferred_element_type=jnp.float32)
        grad_scores = (weights * (grad_probs - row_dots) * score_scale).astype(jnp.bfloat16)
        grad_query = jnp.dot(grad_scores, keys, preferred_element_type=jnp.float32).astype(jnp.bfloat16)
        grad_key = jnp.dot(grad_scores.T, query_rows, preferred_element_type=jnp.float32)
        grad_value = jnp.dot(rounded.T, grad_rows, preferred_element_type=jnp.float32)
        return attended, grad_query, grad_key, grad_value

    attended, grad_query, grad_key, grad_value = lax.map(one_head, (query_heads, grad_heads))
    return (attended.transpose(1, 0, 2).reshape(length, -1),
            grad_query.transpose(1, 0, 2).reshape(length, -1),
            jnp.sum(grad_key, axis=0).astype(jnp.bfloat16),
            jnp.sum(grad_value, axis=0).astype(jnp.bfloat16))


def reference(queries, keys, values, grad_out, doc_lengths, switches):
    results = lax.map(one_sequence, (queries, keys, values, grad_out, doc_lengths))
    where_from = source_index(switches)
    return (jnp.take(results[0], where_from, axis=0),
            jnp.take(results[1], where_from, axis=0),
            jnp.take(results[2], where_from, axis=0),
            jnp.take(results[3], where_from, axis=0))
```

```python
import jax
import jax.numpy as jnp
from jax import lax
from jax.experimental import pallas as pl
from jax.experimental.pallas import tpu as pltpu
from jax.sharding import PartitionSpec as P

NEG_FILL = -1e30


def source_index(switches):
    seq_count = switches.shape[1]
    anchor = jnp.arange(seq_count, dtype=jnp.int32)
    where_from = anchor
    for section_index in range(switches.shape[0]):
        partner = jnp.bitwise_xor(anchor, jnp.int32(1 << section_index))
        where_from = jnp.where(switches[section_index] == 1, where_from[partner], where_from)
    return where_from


def row_starts(lengths, positions):
    ends = jnp.cumsum(lengths)
    starts = ends - lengths
    chosen = jnp.where(starts[None, :] <= positions[:, None], starts[None, :], 0)
    return jnp.max(chosen, axis=1)


def attend(query_rows, grad_rows, keys_all, values_all, allowed, score_scale):
    mask_wide = allowed[:, None, :]
    scores = jnp.where(
        mask_wide,
        jnp.einsum("rhd,cd->rhc", query_rows, keys_all, preferred_element_type=jnp.float32)
        * score_scale,
        NEG_FILL,
    )
    row_max = jnp.max(scores, axis=2, keepdims=True)
    row_sum = jnp.sum(jnp.where(mask_wide, jnp.exp(scores - row_max), 0.0), axis=2, keepdims=True)
    log_total = row_max + jnp.log(row_sum)
    weights = jnp.where(mask_wide, jnp.exp(scores - log_total), 0.0)
    rounded = weights.astype(jnp.bfloat16)
    attended = jnp.einsum(
        "rhc,cd->rhd", rounded, values_all, preferred_element_type=jnp.float32
    ).astype(jnp.bfloat16)
    row_dots = jnp.sum(
        attended.astype(jnp.float32) * grad_rows.astype(jnp.float32), axis=2, keepdims=True
    )
    grad_probs = jnp.einsum(
        "rhd,cd->rhc", grad_rows, values_all, preferred_element_type=jnp.float32
    )
    grad_scores = (weights * (grad_probs - row_dots) * score_scale).astype(jnp.bfloat16)
    grad_query = jnp.einsum(
        "rhc,cd->rhd", grad_scores, keys_all, preferred_element_type=jnp.float32
    ).astype(jnp.bfloat16)
    grad_key = jnp.einsum(
        "rhc,rhd->cd", grad_scores, query_rows, preferred_element_type=jnp.float32
    )
    grad_value = jnp.einsum("rhc,rhd->cd", rounded, grad_rows, preferred_element_type=jnp.float32)
    return (attended, grad_query, grad_key, grad_value)


def body(queries, keys, values, grad_out, doc_lengths, switches):
    home_index = lax.axis_index("dp")
    ctx_index = lax.axis_index("ctx")
    where_from = source_index(switches)
    lengths = lax.dynamic_index_in_dim(doc_lengths, home_index, 0, keepdims=False)
    row_count = queries.shape[1]
    head_size = keys.shape[2]
    head_count = queries.shape[2] // head_size
    head_block = min(4, head_count)
    score_scale = head_size ** (-0.5)
    keys_all, values_all = (
        lax.all_gather(keys[0], "ctx", axis=0, tiled=True),
        lax.all_gather(values[0], "ctx", axis=0, tiled=True),
    )
    length = keys_all.shape[0]
    query_pos = ctx_index * row_count + jnp.arange(row_count, dtype=jnp.int32)
    key_pos = jnp.arange(length, dtype=jnp.int32)
    starts = row_starts(lengths, query_pos)
    allowed = (key_pos[None, :] <= query_pos[:, None]) & (key_pos[None, :] >= starts[:, None])
    query_heads = queries[0].reshape(row_count, head_count, head_size)
    grad_heads = grad_out[0].reshape(row_count, head_count, head_size)
    out_pieces = []
    grad_query_pieces = []
    key_terms = jnp.zeros((length, head_size), jnp.float32)
    value_terms = jnp.zeros((length, head_size), jnp.float32)
    for first_head in range(0, head_count, head_block):
        attended, grad_query, grad_key, grad_value = attend(
            query_heads[:, first_head : first_head + head_block],
            grad_heads[:, first_head : first_head + head_block],
            keys_all,
            values_all,
            allowed,
            score_scale,
        )
        out_pieces.append(attended)
        grad_query_pieces.append(grad_query)
        key_terms = key_terms + grad_key
        value_terms = value_terms + grad_value
    own_keys, own_values = (
        lax.psum_scatter(key_terms, "ctx", scatter_dimension=0, tiled=True),
        lax.psum_scatter(value_terms, "ctx", scatter_dimension=0, tiled=True),
    )
    return relay(
        jnp.concatenate(out_pieces, axis=1).reshape(row_count, head_count * head_size),
        jnp.concatenate(grad_query_pieces, axis=1).reshape(row_count, head_count * head_size),
        own_keys.astype(jnp.bfloat16),
        own_values.astype(jnp.bfloat16),
        where_from,
    )


BF = jnp.bfloat16
MESH = pl.DeviceIdType.MESH


def peer_at(step, me):
    ring, lane = step // 4, step % 4
    half = (ring + 1) // 2
    hop = 8 + jnp.where(ring % 2 == 1, half, -half)
    return ((me // 4 + hop) % 16) * 4 + (me % 4 + lane) % 4


def relay_kernel(
    wf, x, kvx, out_h, dq_h, dk_h, dv_h,
    mid, snd, fin, kvmid, kvsnd, kvfin, ssem, rsem, lsem, osem,
):
    me = lax.axis_index("dp")
    head, part = me // 4, me % 4
    holds = part == head % 4
    barrier = pltpu.get_barrier_semaphore()

    def greet(step, c):
        pl.semaphore_signal(barrier, inc=1, device_id={"dp": peer_at(step, me)}, device_id_type=MESH)
        return c

    lax.fori_loop(0, 60, greet, 0)
    for lane in range(1, 4):
        greet(60 + lane, 0)
    pl.semaphore_wait(barrier, 63)

    def remote(src, dst, which, peer):
        return pltpu.make_async_remote_copy(
            src_ref=src, dst_ref=dst, send_sem=ssem.at[which], recv_sem=rsem.at[which],
            device_id={"dp": peer}, device_id_type=MESH,
        )

    def scatter(step, c):
        p = peer_at(step, me)
        remote(x.at[p], mid.at[me], 0, p).start()
        return c

    lax.fori_loop(0, 60, scatter, 0)
    for lane in range(1, 4):
        scatter(60 + lane, 0)
    own = pltpu.make_async_copy(x.at[me], mid.at[me], lsem.at[0])
    own.start()

    def scatter_kv(i, c):
        t = (head + 8 + i) % 16
        p = 4 * t + t % 4

        @pl.when(p != me)
        def _():
            remote(kvx.at[t], kvmid.at[me], 1, p).start()

        return c

    lax.fori_loop(0, 16, scatter_kv, 0)

    @pl.when(holds)
    def _():
        c = pltpu.make_async_copy(kvx.at[head], kvmid.at[me], lsem.at[1])
        c.start()
        c.wait()
        pltpu.make_async_copy(kvmid.at[pl.ds(0, 63)], kvmid.at[pl.ds(0, 63)], rsem.at[1]).wait()

    own.wait()
    pltpu.make_async_copy(mid.at[pl.ds(0, 63)], mid.at[pl.ds(0, 63)], rsem.at[0]).wait()

    rows = pl.ds(pl.multiple_of(32 * part, 32), 32)
    cols = pl.ds(pl.multiple_of(128 * head, 128), 128)

    def collect(step, c):
        p = peer_at(step, me)
        snd[p] = mid[wf[p]]
        remote(snd.at[p], fin.at[:, rows, cols], 2, p).start()
        return c

    lax.fori_loop(0, 60, collect, 0)
    for lane in range(1, 4):
        collect(60 + lane, 0)
    snd[me] = mid[wf[me]]
    own = pltpu.make_async_copy(snd.at[me], fin.at[:, rows, cols], lsem.at[0])
    own.start()

    @pl.when(holds)
    def _():
        def collect_kv(step, c):
            p = peer_at(step, me)
            kvsnd[p] = kvmid[wf[p]]
            remote(kvsnd.at[p], kvfin.at[head], 3, p).start()
            return c

        lax.fori_loop(0, 60, collect_kv, 0)
        for lane in range(1, 4):
            collect_kv(60 + lane, 0)
        kvsnd[me] = kvmid[wf[me]]
        c = pltpu.make_async_copy(kvsnd.at[me], kvfin.at[head], lsem.at[1])
        c.start()
        c.wait()
        pltpu.make_async_copy(kvfin.at[pl.ds(0, 15)], kvfin.at[pl.ds(0, 15)], rsem.at[3]).wait()

    @pl.when(jnp.logical_not(holds))
    def _():
        pltpu.make_async_copy(kvfin, kvfin, rsem.at[3]).wait()

    own.wait()
    pltpu.make_async_copy(mid.at[pl.ds(0, 63)], mid.at[pl.ds(0, 63)], rsem.at[2]).wait()

    ends = [
        pltpu.make_async_copy(fin.at[0], out_h, osem.at[0]),
        pltpu.make_async_copy(fin.at[1], dq_h, osem.at[1]),
        pltpu.make_async_copy(kvfin.at[pl.ds(0, 8)], dk_h, osem.at[2]),
        pltpu.make_async_copy(kvfin.at[pl.ds(8, 8)], dv_h, osem.at[3]),
    ]
    for c in ends:
        c.start()
    pltpu.make_async_copy(x.at[pl.ds(0, 63)], x.at[pl.ds(0, 63)], ssem.at[0]).wait()
    pltpu.make_async_copy(x.at[pl.ds(0, 63)], x.at[pl.ds(0, 63)], ssem.at[2]).wait()

    @pl.when(holds)
    def _():
        pltpu.make_async_copy(kvmid.at[pl.ds(0, 15)], kvmid.at[pl.ds(0, 15)], ssem.at[1]).wait()
        pltpu.make_async_copy(kvmid.at[pl.ds(0, 63)], kvmid.at[pl.ds(0, 63)], ssem.at[3]).wait()

    @pl.when(jnp.logical_not(holds))
    def _():
        pltpu.make_async_copy(kvmid.at[pl.ds(0, 16)], kvmid.at[pl.ds(0, 16)], ssem.at[1]).wait()

    for c in ends:
        c.wait()


def relay(attended, grad_query, grad_key, grad_value, where_from):
    def pieces(part):
        return part.reshape(4, 32, 16, 128).transpose(2, 0, 1, 3).reshape(64, 32, 128)

    x = jnp.stack([pieces(attended), pieces(grad_query)], axis=1)
    kvx = jnp.concatenate([grad_key.reshape(8, 16, 128), grad_value.reshape(8, 16, 128)], axis=0)
    wide = jax.ShapeDtypeStruct((128, 2048), BF)
    narrow = jax.ShapeDtypeStruct((8, 16, 128), BF)
    vmem = pl.BlockSpec(memory_space=pltpu.VMEM)
    out, dq, dk, dv = pl.pallas_call(
        relay_kernel,
        out_shape=(wide, wide, narrow, narrow),
        in_specs=[pl.BlockSpec(memory_space=pltpu.SMEM), vmem, vmem],
        out_specs=[pl.BlockSpec(memory_space=pl.ANY)] * 4,
        scratch_shapes=[
            pltpu.VMEM((64, 2, 32, 128), BF),
            pltpu.VMEM((64, 2, 32, 128), BF),
            pltpu.VMEM((2, 128, 2048), BF),
            pltpu.VMEM((64, 16, 128), BF),
            pltpu.VMEM((64, 16, 128), BF),
            pltpu.VMEM((16, 16, 128), BF),
            pltpu.SemaphoreType.DMA((4,)),
            pltpu.SemaphoreType.DMA((4,)),
            pltpu.SemaphoreType.DMA((2,)),
            pltpu.SemaphoreType.DMA((4,)),
        ],
        compiler_params=pltpu.CompilerParams(
            collective_id=0, has_side_effects=True, vmem_limit_bytes=32 << 20
        ),
        cost_estimate=pl.CostEstimate(flops=0, bytes_accessed=4 << 20, transcendentals=0),
    )(where_from, x, kvx)
    return (
        out[None], dq[None], dk.reshape(1, 128, 128), dv.reshape(1, 128, 128),
    )


def solution(mesh):
    placed = (
        P("dp", "ctx", None),
        P("dp", "ctx", None),
        P("dp", "ctx", None),
        P("dp", "ctx", None),
        P(),
        P(),
    )
    return jax.shard_map(
        body,
        mesh=mesh,
        in_specs=placed,
        out_specs=(
            P("dp", "ctx", None),
            P("dp", "ctx", None),
            P("dp", "ctx", None),
            P("dp", "ctx", None),
        ),
        check_vma=False,
    )
```

```python
import jax
import jax.numpy as jnp
from jax import lax
from jax.experimental import pallas as pl
from jax.experimental.pallas import tpu as pltpu
from jax.sharding import PartitionSpec as P

NEG_FILL = -1e30
BF = jnp.bfloat16
F32 = jnp.float32
MESH = pl.DeviceIdType.MESH
SCALE = 128 ** (-0.5)
NT = (((1,), (1,)), ((), ()))
NN = (((1,), (0,)), ((), ()))


def dot(a, b, dims):
    return lax.dot_general(a, b, dims, preferred_element_type=F32)


def ring_at(ring, me):
    half = (ring + 1) // 2
    return (me // 4 + 8 + jnp.where(ring % 2 == 1, half, -half)) % 16


def peer_at(step, me):
    return ring_at(step // 4, me) * 4 + (me % 4 + step % 4) % 4


def landed(ref, sem):
    pltpu.make_async_copy(ref, ref, sem).wait()


def kernel(
    lengths, switches, q, k, v, g, out_h, dq_h, dk_h, dv_h,
    kw, vw, kt, vt, bias, dks, dvs, red, x, mid, snd, fin, kvx, kvmid, kvsnd, kvfin, wf,
    ssem, rsem, lsem, osem, gsem, hsem, bsem, csem,
):
    me = lax.axis_index("dp")
    ctx = lax.axis_index("ctx")
    head, part = me // 4, me % 4
    holds = part == head % 4
    barrier = pltpu.get_barrier_semaphore()

    def greet(step, c):
        pl.semaphore_signal(barrier, inc=1, device_id={"dp": peer_at(step, me)}, device_id_type=MESH)
        return c

    for hop in range(1, 5):
        @pl.when(ctx + hop <= 7)
        def _():
            pl.semaphore_signal(barrier, inc=1, device_id={"ctx": ctx + hop}, device_id_type=MESH)

        @pl.when(ctx - hop >= 0)
        def _():
            pl.semaphore_signal(barrier, inc=1, device_id={"ctx": ctx - hop}, device_id_type=MESH)

    lax.fori_loop(0, 60, greet, 0)
    for lane in range(1, 4):
        greet(60 + lane, 0)
    pl.semaphore_wait(barrier, 63 + jnp.minimum(ctx, 4) + jnp.minimum(7 - ctx, 4))

    def to_ctx(src, dst, send, recv, peer):
        return pltpu.make_async_remote_copy(
            src_ref=src, dst_ref=dst, send_sem=send, recv_sem=recv,
            device_id={"ctx": peer}, device_id_type=MESH,
        )

    def to_dp(src, dst, which, peer):
        return pltpu.make_async_remote_copy(
            src_ref=src, dst_ref=dst, send_sem=ssem.at[which], recv_sem=rsem.at[which],
            device_id={"dp": peer}, device_id_type=MESH,
        )

    for hop in range(1, 5):
        rows = pl.ds(128 * (4 - hop), 128)

        @pl.when(ctx + hop <= 7)
        def _():
            to_ctx(k, kw.at[rows], gsem.at[hop - 1], hsem.at[hop - 1], ctx + hop).start()
            to_ctx(v, vw.at[rows], gsem.at[hop + 3], hsem.at[hop + 3], ctx + hop).start()

        @pl.when(ctx - hop < 0)
        def _():
            kw[rows] = jnp.zeros((128, 128), BF)
            vw[rows] = jnp.zeros((128, 128), BF)

    kw[pl.ds(512, 128)] = k[...]
    vw[pl.ds(512, 128)] = v[...]
    dks[...] = jnp.zeros_like(dks)
    dvs[...] = jnp.zeros_like(dvs)

    row_pos = 128 * ctx + lax.broadcasted_iota(jnp.int32, (1, 256), 1) % 128
    key_pos = 128 * (ctx - 4) + lax.broadcasted_iota(jnp.int32, (640, 256), 0)
    first = jnp.int32(0)
    starts = jnp.zeros((1, 256), jnp.int32)
    for doc in range(8):
        starts = jnp.where(first <= row_pos, jnp.maximum(starts, first), starts)
        first = first + lengths[me, doc]
    bias[...] = jnp.where((key_pos <= row_pos) & (key_pos >= starts), 0.0, NEG_FILL)

    def begin(r, c):
        wf[0, r] = r
        return c

    lax.fori_loop(0, 64, begin, 0)
    for bit in range(6):
        def section(r, c):
            size = 1 << bit
            other = r + size * (1 - 2 * ((r // size) % 2))
            wf[bit + 1, r] = jnp.where(switches[bit, r] == 1, wf[bit, other], wf[bit, r])
            return c

        lax.fori_loop(0, 64, section, 0)

    for hop in range(1, 5):
        @pl.when(ctx - hop >= 0)
        def _():
            landed(k, hsem.at[hop - 1])
            landed(v, hsem.at[hop + 3])

    kt[...] = kw[...].astype(F32).T.astype(BF)
    vt[...] = vw[...].astype(F32).T.astype(BF)

    def pair(i, c):
        ha, hb = ring_at(2 * i, me), ring_at(2 * i + 1, me)
        ca = pl.ds(pl.multiple_of(128 * ha, 128), 128)
        cb = pl.ds(pl.multiple_of(128 * hb, 128), 128)
        q2 = jnp.concatenate([q[:, ca], q[:, cb]], axis=0)
        g2 = jnp.concatenate([g[:, ca], g[:, cb]], axis=0)
        s = dot(kw[...], q2, NT) * SCALE + bias[...]
        e = jnp.exp(s - jnp.max(s, axis=0, keepdims=True))
        w = e * (1.0 / jnp.sum(e, axis=0, keepdims=True))
        rounded = w.astype(BF)
        ot = dot(vt[...], rounded, NN).astype(BF).astype(F32)
        dots = jnp.sum(ot * g2.astype(F32).T, axis=0, keepdims=True)
        ds = (w * (dot(vw[...], g2, NT) - dots) * SCALE).astype(BF)
        dqt = dot(kt[...], ds, NN)
        dks[...] += dot(ds, q2, NN)
        dvs[...] += dot(rounded, g2, NN)
        o = ot.T.astype(BF).reshape(8, 32, 128)
        dq = dqt.T.astype(BF).reshape(8, 32, 128)
        for n in range(4):
            x[4 * ha + n, 0] = o[n]
            x[4 * ha + n, 1] = dq[n]
            x[4 * hb + n, 0] = o[4 + n]
            x[4 * hb + n, 1] = dq[4 + n]
        for n in range(8):
            p = peer_at(8 * i + n, me)

            @pl.when(p != me)
            def _():
                to_dp(x.at[p], mid.at[me], 0, p).start()

        return c

    lax.fori_loop(0, 8, pair, 0)
    own = pltpu.make_async_copy(x.at[me], mid.at[me], lsem.at[0])
    own.start()

    for hop in range(1, 5):
        rows = pl.ds(128 * (4 - hop), 128)

        @pl.when(ctx - hop >= 0)
        def _():
            to_ctx(dks.at[rows], red.at[hop - 1, 0], bsem.at[hop - 1], csem.at[hop - 1], ctx - hop).start()
            to_ctx(dvs.at[rows], red.at[hop - 1, 1], bsem.at[hop + 3], csem.at[hop + 3], ctx - hop).start()

        @pl.when(ctx + hop > 7)
        def _():
            red[hop - 1] = jnp.zeros((2, 128, 128), F32)

    for hop in range(1, 5):
        @pl.when(ctx + hop <= 7)
        def _():
            landed(red.at[hop - 1, 0], csem.at[hop - 1])
            landed(red.at[hop - 1, 1], csem.at[hop + 3])

    total_k = dks[pl.ds(512, 128)] + ((red[0, 0] + red[1, 0]) + (red[2, 0] + red[3, 0]))
    total_v = dvs[pl.ds(512, 128)] + ((red[0, 1] + red[1, 1]) + (red[2, 1] + red[3, 1]))
    kvx[pl.ds(0, 8)] = total_k.astype(BF).reshape(8, 16, 128)
    kvx[pl.ds(8, 8)] = total_v.astype(BF).reshape(8, 16, 128)

    def scatter_kv(i, c):
        t = (head + 8 + i) % 16
        p = 4 * t + t % 4

        @pl.when(p != me)
        def _():
            to_dp(kvx.at[t], kvmid.at[me], 1, p).start()

        return c

    lax.fori_loop(0, 16, scatter_kv, 0)

    @pl.when(holds)
    def _():
        c = pltpu.make_async_copy(kvx.at[head], kvmid.at[me], lsem.at[1])
        c.start()
        c.wait()
        landed(kvmid.at[pl.ds(0, 63)], rsem.at[1])

    own.wait()
    landed(mid.at[pl.ds(0, 63)], rsem.at[0])

    rows = pl.ds(pl.multiple_of(32 * part, 32), 32)
    cols = pl.ds(pl.multiple_of(128 * head, 128), 128)

    def collect(step, c):
        p = peer_at(step, me)
        snd[p] = mid[wf[6, p]]
        to_dp(snd.at[p], fin.at[:, rows, cols], 2, p).start()
        return c

    lax.fori_loop(0, 60, collect, 0)
    for lane in range(1, 4):
        collect(60 + lane, 0)
    snd[me] = mid[wf[6, me]]
    own = pltpu.make_async_copy(snd.at[me], fin.at[:, rows, cols], lsem.at[0])
    own.start()

    @pl.when(holds)
    def _():
        def collect_kv(step, c):
            p = peer_at(step, me)
            kvsnd[p] = kvmid[wf[6, p]]
            to_dp(kvsnd.at[p], kvfin.at[head], 3, p).start()
            return c

        lax.fori_loop(0, 60, collect_kv, 0)
        for lane in range(1, 4):
            collect_kv(60 + lane, 0)
        kvsnd[me] = kvmid[wf[6, me]]
        c = pltpu.make_async_copy(kvsnd.at[me], kvfin.at[head], lsem.at[1])
        c.start()
        c.wait()
        landed(kvfin.at[pl.ds(0, 15)], rsem.at[3])

    @pl.when(jnp.logical_not(holds))
    def _():
        landed(kvfin, rsem.at[3])

    own.wait()
    landed(mid.at[pl.ds(0, 63)], rsem.at[2])

    ends = [
        pltpu.make_async_copy(fin.at[0], out_h, osem.at[0]),
        pltpu.make_async_copy(fin.at[1], dq_h, osem.at[1]),
        pltpu.make_async_copy(kvfin.at[pl.ds(0, 8)], dk_h, osem.at[2]),
        pltpu.make_async_copy(kvfin.at[pl.ds(8, 8)], dv_h, osem.at[3]),
    ]
    for c in ends:
        c.start()
    landed(x.at[pl.ds(0, 63)], ssem.at[0])
    landed(x.at[pl.ds(0, 63)], ssem.at[2])

    @pl.when(holds)
    def _():
        landed(kvmid.at[pl.ds(0, 15)], ssem.at[1])
        landed(kvmid.at[pl.ds(0, 63)], ssem.at[3])

    @pl.when(jnp.logical_not(holds))
    def _():
        landed(kvmid.at[pl.ds(0, 16)], ssem.at[1])

    for hop in range(1, 5):
        @pl.when(ctx + hop <= 7)
        def _():
            landed(k, gsem.at[hop - 1])
            landed(v, gsem.at[hop + 3])

        @pl.when(ctx - hop >= 0)
        def _():
            landed(red.at[hop - 1, 0], bsem.at[hop - 1])
            landed(red.at[hop - 1, 1], bsem.at[hop + 3])

    for c in ends:
        c.wait()


def body(queries, keys, values, grad_out, doc_lengths, switches):
    wide = jax.ShapeDtypeStruct((128, 2048), BF)
    narrow = jax.ShapeDtypeStruct((8, 16, 128), BF)
    smem = pl.BlockSpec(memory_space=pltpu.SMEM)
    vmem = pl.BlockSpec(memory_space=pltpu.VMEM)
    dma = pltpu.SemaphoreType.DMA
    out, dq, dk, dv = pl.pallas_call(
        kernel,
        out_shape=(wide, wide, narrow, narrow),
        in_specs=[smem, smem, vmem, vmem, vmem, vmem],
        out_specs=[pl.BlockSpec(memory_space=pl.ANY)] * 4,
        scratch_shapes=[
            pltpu.VMEM((640, 128), BF),
            pltpu.VMEM((640, 128), BF),
            pltpu.VMEM((128, 640), BF),
            pltpu.VMEM((128, 640), BF),
            pltpu.VMEM((640, 256), F32),
            pltpu.VMEM((640, 128), F32),
            pltpu.VMEM((640, 128), F32),
            pltpu.VMEM((4, 2, 128, 128), F32),
            pltpu.VMEM((64, 2, 32, 128), BF),
            pltpu.VMEM((64, 2, 32, 128), BF),
            pltpu.VMEM((64, 2, 32, 128), BF),
            pltpu.VMEM((2, 128, 2048), BF),
            pltpu.VMEM((16, 16, 128), BF),
            pltpu.VMEM((64, 16, 128), BF),
            pltpu.VMEM((64, 16, 128), BF),
            pltpu.VMEM((16, 16, 128), BF),
            pltpu.SMEM((7, 64), jnp.int32),
            dma((4,)), dma((4,)), dma((2,)), dma((4,)),
            dma((8,)), dma((8,)), dma((8,)), dma((8,)),
        ],
        compiler_params=pltpu.CompilerParams(
            collective_id=0, has_side_effects=True, vmem_limit_bytes=32 << 20
        ),
        cost_estimate=pl.CostEstimate(
            flops=2_000_000_000, bytes_accessed=4 << 20, transcendentals=1_300_000
        ),
    )(doc_lengths, switches, queries[0], keys[0], values[0], grad_out[0])
    return (out[None], dq[None], dk.reshape(1, 128, 128), dv.reshape(1, 128, 128))


def solution(mesh):
    split = P("dp", "ctx", None)
    return jax.shard_map(
        body,
        mesh=mesh,
        in_specs=(split, split, split, split, P(), P()),
        out_specs=(split, split, split, split),
        check_vma=False,
    )
```

```python
import jax
import jax.numpy as jnp
from jax import lax
from jax.experimental import pallas as pl
from jax.experimental.pallas import tpu as pltpu
from jax.sharding import PartitionSpec as P

NEG_FILL = -1e30
BF = jnp.bfloat16
F32 = jnp.float32
MESH = pl.DeviceIdType.MESH
SCALE = 128 ** (-0.5)
NT = (((1,), (1,)), ((), ()))
NN = (((1,), (0,)), ((), ()))


def dot(a, b, dims):
    return lax.dot_general(a, b, dims, preferred_element_type=F32)


def ring_at(ring, me):
    half = (ring + 1) // 2
    return (me // 4 + 8 + jnp.where(ring % 2 == 1, half, -half)) % 16


def plane_at(ring, me):
    group = ring // 4
    group = group + jnp.where(group == 2, 1, jnp.where(group == 3, -1, 0))
    return 4 * group + (ring + me // 4) % 4


def peer_at(step, me):
    return plane_at(step // 4, me) * 4 + (me % 4 + step) % 4


def landed(ref, sem):
    pltpu.make_async_copy(ref, ref, sem).wait()


def kernel(
    lengths_h, switches_h, q_h, k, v, g_h, fin, kvfin,
    q, g, kw, vw, kt, vt, bias, dks, dvs, red, x, mid, snd, kvx, kvmid, kvsnd, lengths, switches, wf,
    ssem, rsem, lsem, isem, gsem, hsem, bsem, csem,
):
    me = lax.axis_index("dp")
    ctx = lax.axis_index("ctx")
    head, part = me // 4, me % 4
    holds = part == head % 4
    barrier = pltpu.get_barrier_semaphore()
    fetches = [
        pltpu.make_async_copy(k, kw.at[pl.ds(512, 128)], isem.at[0]),
        pltpu.make_async_copy(v, vw.at[pl.ds(512, 128)], isem.at[1]),
        pltpu.make_async_copy(q_h, q, isem.at[2]),
        pltpu.make_async_copy(g_h, g, isem.at[3]),
        pltpu.make_async_copy(lengths_h, lengths, isem.at[4]),
        pltpu.make_async_copy(switches_h, switches, isem.at[5]),
    ]
    for c in fetches:
        c.start()

    def greet(step, c):
        pl.semaphore_signal(
            barrier, inc=1, device_id={"dp": (me + step) % 64}, device_id_type=MESH
        )
        return c

    for hop in range(1, 5):
        @pl.when(ctx + hop <= 7)
        def _():
            pl.semaphore_signal(barrier, inc=1, device_id={"ctx": ctx + hop}, device_id_type=MESH)

        @pl.when(ctx - hop >= 0)
        def _():
            pl.semaphore_signal(barrier, inc=1, device_id={"ctx": ctx - hop}, device_id_type=MESH)

    lax.fori_loop(1, 64, greet, 0)
    pl.semaphore_wait(barrier, 63 + jnp.minimum(ctx, 4) + jnp.minimum(7 - ctx, 4))

    def to_ctx(src, dst, send, recv, peer):
        return pltpu.make_async_remote_copy(
            src_ref=src, dst_ref=dst, send_sem=send, recv_sem=recv,
            device_id={"ctx": peer}, device_id_type=MESH,
        )

    def to_dp(src, dst, which, peer):
        return pltpu.make_async_remote_copy(
            src_ref=src, dst_ref=dst, send_sem=ssem.at[which], recv_sem=rsem.at[which],
            device_id={"dp": peer}, device_id_type=MESH,
        )

    for hop in range(1, 5):
        rows = pl.ds(128 * (4 - hop), 128)

        @pl.when(ctx + hop <= 7)
        def _():
            to_ctx(k, kw.at[rows], gsem.at[hop - 1], hsem.at[hop - 1], ctx + hop).start()
            to_ctx(v, vw.at[rows], gsem.at[hop + 3], hsem.at[hop + 3], ctx + hop).start()

    for c in fetches:
        c.wait()

    row_pos = 128 * ctx + lax.broadcasted_iota(jnp.int32, (1, 256), 1) % 128
    key_pos = 128 * (ctx - 4) + lax.broadcasted_iota(jnp.int32, (640, 256), 0)
    first = jnp.int32(0)
    starts = jnp.zeros((1, 256), jnp.int32)
    for doc in range(8):
        starts = jnp.where(first <= row_pos, jnp.maximum(starts, first), starts)
        first = first + lengths[doc, me]
    bias[...] = jnp.where((key_pos <= row_pos) & (key_pos >= starts), 0.0, NEG_FILL)

    dks[...] = jnp.zeros_like(dks)
    dvs[...] = jnp.zeros_like(dvs)
    for hop in range(1, 5):
        rows = pl.ds(128 * (4 - hop), 128)

        @pl.when(ctx - hop < 0)
        def _():
            kw[rows] = jnp.zeros((128, 128), BF)
            vw[rows] = jnp.zeros((128, 128), BF)

    for hop in range(1, 5):
        @pl.when(ctx - hop >= 0)
        def _():
            landed(k, hsem.at[hop - 1])
            landed(v, hsem.at[hop + 3])

    kt[...] = kw[...].T
    vt[...] = vw[...].T

    def pair(i, c):
        ha, hb = ring_at(2 * i, me), ring_at(2 * i + 1, me)
        ca = pl.ds(pl.multiple_of(128 * ha, 128), 128)
        cb = pl.ds(pl.multiple_of(128 * hb, 128), 128)
        q2 = jnp.concatenate([q[:, ca], q[:, cb]], axis=0)
        g2 = jnp.concatenate([g[:, ca], g[:, cb]], axis=0)
        s = dot(kw[...], q2, NT) * SCALE + bias[...]
        e = jnp.exp(s - jnp.max(s, axis=0, keepdims=True))
        w = e * (1.0 / jnp.sum(e, axis=0, keepdims=True))
        rounded = w.astype(BF)
        ot = dot(vt[...], rounded, NN).astype(BF).astype(F32)
        dots = jnp.sum(ot * g2.astype(F32).T, axis=0, keepdims=True)
        ds = (w * (dot(vw[...], g2, NT) - dots) * SCALE).astype(BF)
        dqt = dot(kt[...], ds, NN)
        dks[...] += dot(ds, q2, NN)
        dvs[...] += dot(rounded, g2, NN)
        o = ot.T.astype(BF).reshape(8, 32, 128)
        dq = dqt.T.astype(BF).reshape(8, 32, 128)
        for n in range(4):
            x[4 * ha + n, 0] = o[n]
            x[4 * ha + n, 1] = dq[n]
            x[4 * hb + n, 0] = o[4 + n]
            x[4 * hb + n, 1] = dq[4 + n]
        for n in range(8):
            p = ring_at((8 * i + n) // 4, me) * 4 + (me % 4 + n) % 4

            @pl.when(p != me)
            def _():
                to_dp(x.at[p], mid.at[me], 0, p).start()

        return c

    lax.fori_loop(0, 8, pair, 0)
    own = pltpu.make_async_copy(x.at[me], mid.at[me], lsem.at[0])
    own.start()

    for hop in range(1, 5):
        rows = pl.ds(128 * (4 - hop), 128)

        @pl.when(ctx - hop >= 0)
        def _():
            to_ctx(dks.at[rows], red.at[hop - 1, 0], bsem.at[hop - 1], csem.at[hop - 1], ctx - hop).start()
            to_ctx(dvs.at[rows], red.at[hop - 1, 1], bsem.at[hop + 3], csem.at[hop + 3], ctx - hop).start()

        @pl.when(ctx + hop > 7)
        def _():
            red[hop - 1] = jnp.zeros((2, 128, 128), F32)

    def begin(r, c):
        wf[0, r] = r
        return c

    lax.fori_loop(0, 64, begin, 0)
    for bit in range(6):
        def section(r, c):
            size = 1 << bit
            other = r + size * (1 - 2 * ((r // size) % 2))
            wf[bit + 1, r] = jnp.where(switches[bit, r] == 1, wf[bit, other], wf[bit, r])
            return c

        lax.fori_loop(0, 64, section, 0)

    for hop in range(1, 5):
        @pl.when(ctx + hop <= 7)
        def _():
            landed(red.at[hop - 1, 0], csem.at[hop - 1])
            landed(red.at[hop - 1, 1], csem.at[hop + 3])

    total_k = dks[pl.ds(512, 128)] + ((red[0, 0] + red[1, 0]) + (red[2, 0] + red[3, 0]))
    total_v = dvs[pl.ds(512, 128)] + ((red[0, 1] + red[1, 1]) + (red[2, 1] + red[3, 1]))
    kvx[pl.ds(0, 8)] = total_k.astype(BF).reshape(8, 16, 128)
    kvx[pl.ds(8, 8)] = total_v.astype(BF).reshape(8, 16, 128)

    def scatter_kv(i, c):
        t = (head + 8 + i) % 16
        p = 4 * t + t % 4

        @pl.when(p != me)
        def _():
            to_dp(kvx.at[t], kvmid.at[me], 1, p).start()

        return c

    lax.fori_loop(0, 16, scatter_kv, 0)

    @pl.when(holds)
    def _():
        c = pltpu.make_async_copy(kvx.at[head], kvmid.at[me], lsem.at[1])
        c.start()
        c.wait()
        landed(kvmid.at[pl.ds(0, 63)], rsem.at[1])

    own.wait()
    landed(mid.at[pl.ds(0, 63)], rsem.at[0])

    rows = pl.ds(pl.multiple_of(32 * part, 32), 32)
    cols = pl.ds(pl.multiple_of(128 * head, 128), 128)

    def collect(step, c):
        p = peer_at(step, me)
        snd[p] = mid[wf[6, p]]

        @pl.when(p != me)
        def _():
            to_dp(snd.at[p], fin.at[:, rows, cols], 2, p).start()

        @pl.when(holds)
        def _():
            kvsnd[p] = kvmid[wf[6, p]]

            @pl.when(p != me)
            def _():
                to_dp(kvsnd.at[p], kvfin.at[head], 3, p).start()

        return c

    lax.fori_loop(0, 64, collect, 0)
    own = pltpu.make_async_copy(snd.at[me], fin.at[:, rows, cols], lsem.at[0])
    own.start()

    @pl.when(holds)
    def _():
        c = pltpu.make_async_copy(kvsnd.at[me], kvfin.at[head], lsem.at[1])
        c.start()
        c.wait()
        landed(kvfin.at[pl.ds(0, 15)], rsem.at[3])

    @pl.when(jnp.logical_not(holds))
    def _():
        landed(kvfin, rsem.at[3])

    own.wait()
    landed(mid.at[pl.ds(0, 63)], rsem.at[2])

    landed(x.at[pl.ds(0, 63)], ssem.at[0])
    landed(x.at[pl.ds(0, 63)], ssem.at[2])

    @pl.when(holds)
    def _():
        landed(kvmid.at[pl.ds(0, 15)], ssem.at[1])
        landed(kvmid.at[pl.ds(0, 63)], ssem.at[3])

    @pl.when(jnp.logical_not(holds))
    def _():
        landed(kvmid.at[pl.ds(0, 16)], ssem.at[1])

    for hop in range(1, 5):
        @pl.when(ctx + hop <= 7)
        def _():
            landed(k, gsem.at[hop - 1])
            landed(v, gsem.at[hop + 3])

        @pl.when(ctx - hop >= 0)
        def _():
            landed(red.at[hop - 1, 0], bsem.at[hop - 1])
            landed(red.at[hop - 1, 1], bsem.at[hop + 3])


def place_kernel(fin, kvfin, out_h, dq_h, dk_h, dv_h, sem):
    ends = [
        pltpu.make_async_copy(fin.at[0], out_h, sem.at[0]),
        pltpu.make_async_copy(fin.at[1], dq_h, sem.at[1]),
        pltpu.make_async_copy(kvfin.at[pl.ds(0, 8)], dk_h, sem.at[2]),
        pltpu.make_async_copy(kvfin.at[pl.ds(8, 8)], dv_h, sem.at[3]),
    ]
    for c in ends:
        c.start()
    for c in ends:
        c.wait()


def body(queries, keys, values, grad_out, doc_lengths, switches):
    wide = jax.ShapeDtypeStruct((128, 2048), BF)
    narrow = jax.ShapeDtypeStruct((8, 16, 128), BF)
    vmem = pl.BlockSpec(memory_space=pltpu.VMEM)
    hbm = pl.BlockSpec(memory_space=pltpu.HBM)
    dma = pltpu.SemaphoreType.DMA
    fin, kvfin = pl.pallas_call(
        kernel,
        out_shape=(
            jax.ShapeDtypeStruct((2, 128, 2048), BF),
            jax.ShapeDtypeStruct((16, 16, 128), BF),
        ),
        in_specs=[hbm] * 6,
        out_specs=[vmem, vmem],
        scratch_shapes=[
            pltpu.VMEM((128, 2048), BF),
            pltpu.VMEM((128, 2048), BF),
            pltpu.VMEM((640, 128), BF),
            pltpu.VMEM((640, 128), BF),
            pltpu.VMEM((128, 640), BF),
            pltpu.VMEM((128, 640), BF),
            pltpu.VMEM((640, 256), F32),
            pltpu.VMEM((640, 128), F32),
            pltpu.VMEM((640, 128), F32),
            pltpu.VMEM((4, 2, 128, 128), F32),
            pltpu.VMEM((64, 2, 32, 128), BF),
            pltpu.VMEM((64, 2, 32, 128), BF),
            pltpu.VMEM((64, 2, 32, 128), BF),
            pltpu.VMEM((16, 16, 128), BF),
            pltpu.VMEM((64, 16, 128), BF),
            pltpu.VMEM((64, 16, 128), BF),
            pltpu.SMEM((8, 64), jnp.int32),
            pltpu.SMEM((6, 64), jnp.int32),
            pltpu.SMEM((7, 64), jnp.int32),
            dma((4,)), dma((4,)), dma((2,)), dma((6,)),
            dma((8,)), dma((8,)), dma((8,)), dma((8,)),
        ],
        compiler_params=pltpu.CompilerParams(
            collective_id=0, has_side_effects=True, vmem_limit_bytes=60 << 20
        ),
        cost_estimate=pl.CostEstimate(
            flops=2_000_000_000, bytes_accessed=4 << 20, transcendentals=1_300_000
        ),
    )(doc_lengths.T, switches, queries[0], keys[0], values[0], grad_out[0])
    out, dq, dk, dv = pl.pallas_call(
        place_kernel,
        out_shape=(wide, wide, narrow, narrow),
        in_specs=[vmem, vmem],
        out_specs=[hbm] * 4,
        scratch_shapes=[dma((4,))],
        cost_estimate=pl.CostEstimate(flops=0, bytes_accessed=2 << 20, transcendentals=0),
    )(fin, kvfin)
    return (out[None], dq[None], dk.reshape(1, 128, 128), dv.reshape(1, 128, 128))


def solution(mesh):
    split = P("dp", "ctx", None)
    return jax.shard_map(
        body,
        mesh=mesh,
        in_specs=(split, split, split, split, P(), P()),
        out_specs=(split, split, split, split),
        check_vma=False,
    )
```

```python
import jax
import jax.numpy as jnp
from jax import lax
from jax.experimental import pallas as pl
from jax.experimental.pallas import tpu as pltpu
from jax.sharding import PartitionSpec as P

NEG_FILL = -1e30
BF = jnp.bfloat16
F32 = jnp.float32
MESH = pl.DeviceIdType.MESH
SCALE = 128 ** (-0.5)
NT = (((1,), (1,)), ((), ()))
NN = (((1,), (0,)), ((), ()))


def dot(a, b, dims):
    return lax.dot_general(a, b, dims, preferred_element_type=F32)


def ring_at(ring, me):
    half = (ring + 1) // 2
    return (me // 4 + 8 + jnp.where(ring % 2 == 1, half, -half)) % 16


def plane_at(ring, me):
    group = ring // 4
    group = group + jnp.where(group == 2, 1, jnp.where(group == 3, -1, 0))
    return 4 * group + (ring + me // 4) % 4


def peer_at(step, me):
    return plane_at(step // 4, me) * 4 + (me % 4 + step) % 4


def landed(ref, sem):
    pltpu.make_async_copy(ref, ref, sem).wait()


def kernel(
    lengths_h, switches_h, q_h, k, v, g_h, fin, kvfin,
    q, g, kw, vw, kt, vt, bias, dks, dvs, red, x, mid, snd, kvx, kvmid, kvsnd, lengths, switches, wf,
    ssem, rsem, lsem, isem, gsem, hsem, bsem, csem, ready,
):
    me = lax.axis_index("dp")
    ctx = lax.axis_index("ctx")
    head, part = me // 4, me % 4
    holds = part == head % 4
    barrier = pltpu.get_barrier_semaphore()
    fetches = [
        pltpu.make_async_copy(k, kw.at[pl.ds(512, 128)], isem.at[0]),
        pltpu.make_async_copy(v, vw.at[pl.ds(512, 128)], isem.at[1]),
        pltpu.make_async_copy(q_h, q, isem.at[2]),
        pltpu.make_async_copy(g_h, g, isem.at[3]),
        pltpu.make_async_copy(lengths_h, lengths, isem.at[4]),
        pltpu.make_async_copy(switches_h, switches, isem.at[5]),
    ]
    for c in fetches:
        c.start()

    def greet(p):
        pl.semaphore_signal(barrier, inc=1, device_id={"dp": p}, device_id_type=MESH)

    def greet_column(step, c):
        greet((me + 4 * step) % 64)
        return c

    def neighbour(lane):
        return 4 * head + (part + lane) % 4

    lax.fori_loop(1, 16, greet_column, 0)
    for lane in range(1, 4):
        greet(neighbour(lane))
    for hop in range(1, 5):
        @pl.when(ctx + hop <= 7)
        def _():
            pl.semaphore_signal(barrier, inc=1, device_id={"ctx": ctx + hop}, device_id_type=MESH)

        @pl.when(ctx - hop >= 0)
        def _():
            pl.semaphore_signal(barrier, inc=1, device_id={"ctx": ctx - hop}, device_id_type=MESH)

    pl.semaphore_wait(barrier, 18 + jnp.minimum(ctx, 4) + jnp.minimum(7 - ctx, 4))

    def to_ctx(src, dst, send, recv, peer):
        return pltpu.make_async_remote_copy(
            src_ref=src, dst_ref=dst, send_sem=send, recv_sem=recv,
            device_id={"ctx": peer}, device_id_type=MESH,
        )

    def to_dp(src, dst, which, peer):
        return pltpu.make_async_remote_copy(
            src_ref=src, dst_ref=dst, send_sem=ssem.at[which], recv_sem=rsem.at[which],
            device_id={"dp": peer}, device_id_type=MESH,
        )

    for ref, place, base in ((k, kw, 0), (v, vw, 4)):
        for hop in range(1, 5):
            @pl.when(ctx + hop <= 7)
            def _():
                to_ctx(
                    ref, place.at[pl.ds(128 * (4 - hop), 128)], gsem.at[base + hop - 1],
                    hsem.at[base + hop - 1], ctx + hop,
                ).start()

    for lane in range(1, 4):
        pl.semaphore_signal(
            ready, inc=1, device_id={"dp": neighbour(lane)}, device_id_type=MESH
        )

    for c in fetches:
        c.wait()

    row_pos = 128 * ctx + lax.broadcasted_iota(jnp.int32, (1, 256), 1) % 128
    key_pos = 128 * (ctx - 4) + lax.broadcasted_iota(jnp.int32, (640, 256), 0)
    first = jnp.int32(0)
    starts = jnp.zeros((1, 256), jnp.int32)
    for doc in range(8):
        starts = jnp.where(first <= row_pos, jnp.maximum(starts, first), starts)
        first = first + lengths[doc, me]
    bias[...] = jnp.where((key_pos <= row_pos) & (key_pos >= starts), 0.0, NEG_FILL)

    dks[...] = jnp.zeros_like(dks)
    dvs[...] = jnp.zeros_like(dvs)
    for hop in range(1, 5):
        rows = pl.ds(128 * (4 - hop), 128)

        @pl.when(ctx - hop < 0)
        def _():
            kw[rows] = jnp.zeros((128, 128), BF)
            vw[rows] = jnp.zeros((128, 128), BF)

    for hop in range(1, 5):
        @pl.when(ctx - hop >= 0)
        def _():
            landed(k, hsem.at[hop - 1])

    pl.semaphore_wait(ready, 3)

    def pair(i, c):
        ha, hb = ring_at(2 * i, me), ring_at(2 * i + 1, me)
        ca = pl.ds(pl.multiple_of(128 * ha, 128), 128)
        cb = pl.ds(pl.multiple_of(128 * hb, 128), 128)
        q2 = jnp.concatenate([q[:, ca], q[:, cb]], axis=0)
        g2 = jnp.concatenate([g[:, ca], g[:, cb]], axis=0)
        s = dot(kw[...], q2, NT) * SCALE + bias[...]
        e = jnp.exp(s - jnp.max(s, axis=0, keepdims=True))
        w = e * (1.0 / jnp.sum(e, axis=0, keepdims=True))
        rounded = w.astype(BF)

        @pl.when(i == 0)
        def _():
            kt[...] = kw[...].T
            for hop in range(1, 5):
                @pl.when(ctx - hop >= 0)
                def _():
                    landed(v, hsem.at[hop + 3])

            vt[...] = vw[...].T

        ot = dot(vt[...], rounded, NN).astype(BF).astype(F32)
        dots = jnp.sum(ot * g2.astype(F32).T, axis=0, keepdims=True)
        ds = (w * (dot(vw[...], g2, NT) - dots) * SCALE).astype(BF)
        dqt = dot(kt[...], ds, NN)
        dks[...] += dot(ds, q2, NN)
        dvs[...] += dot(rounded, g2, NN)
        o = ot.T.astype(BF).reshape(8, 32, 128)
        dq = dqt.T.astype(BF).reshape(8, 32, 128)
        for n in range(4):
            x[4 * ha + n, 0] = o[n]
            x[4 * ha + n, 1] = dq[n]
            x[4 * hb + n, 0] = o[4 + n]
            x[4 * hb + n, 1] = dq[4 + n]
        for n in range(8):
            p = ring_at((8 * i + n) // 4, me) * 4 + (me % 4 + n) % 4

            @pl.when(p != me)
            def _():
                to_dp(x.at[p], mid.at[me], 0, p).start()

        return c

    lax.fori_loop(0, 8, pair, 0)
    own = pltpu.make_async_copy(x.at[me], mid.at[me], lsem.at[0])
    own.start()

    for hop in range(1, 5):
        rows = pl.ds(128 * (4 - hop), 128)

        @pl.when(ctx - hop >= 0)
        def _():
            to_ctx(dks.at[rows], red.at[hop - 1, 0], bsem.at[hop - 1], csem.at[hop - 1], ctx - hop).start()
            to_ctx(dvs.at[rows], red.at[hop - 1, 1], bsem.at[hop + 3], csem.at[hop + 3], ctx - hop).start()

        @pl.when(ctx + hop > 7)
        def _():
            red[hop - 1] = jnp.zeros((2, 128, 128), F32)

    def begin(r, c):
        wf[0, r] = r
        return c

    lax.fori_loop(0, 64, begin, 0)
    for bit in range(6):
        def section(r, c):
            size = 1 << bit
            other = r + size * (1 - 2 * ((r // size) % 2))
            wf[bit + 1, r] = jnp.where(switches[bit, r] == 1, wf[bit, other], wf[bit, r])
            return c

        lax.fori_loop(0, 64, section, 0)

    for hop in range(1, 5):
        @pl.when(ctx + hop <= 7)
        def _():
            landed(red.at[hop - 1, 0], csem.at[hop - 1])
            landed(red.at[hop - 1, 1], csem.at[hop + 3])

    total_k = dks[pl.ds(512, 128)] + ((red[0, 0] + red[1, 0]) + (red[2, 0] + red[3, 0]))
    total_v = dvs[pl.ds(512, 128)] + ((red[0, 1] + red[1, 1]) + (red[2, 1] + red[3, 1]))
    kvx[pl.ds(0, 8)] = total_k.astype(BF).reshape(8, 16, 128)
    kvx[pl.ds(8, 8)] = total_v.astype(BF).reshape(8, 16, 128)

    def scatter_kv(i, c):
        t = (head + 8 + i) % 16
        p = 4 * t + t % 4

        @pl.when(p != me)
        def _():
            to_dp(kvx.at[t], kvmid.at[me], 1, p).start()

        return c

    lax.fori_loop(0, 16, scatter_kv, 0)

    @pl.when(holds)
    def _():
        c = pltpu.make_async_copy(kvx.at[head], kvmid.at[me], lsem.at[1])
        c.start()
        c.wait()
        landed(kvmid.at[pl.ds(0, 63)], rsem.at[1])

    own.wait()
    landed(mid.at[pl.ds(0, 63)], rsem.at[0])

    rows = pl.ds(pl.multiple_of(32 * part, 32), 32)
    cols = pl.ds(pl.multiple_of(128 * head, 128), 128)

    def collect(step, c):
        p = peer_at(step, me)
        snd[p] = mid[wf[6, p]]

        @pl.when(p != me)
        def _():
            to_dp(snd.at[p], fin.at[:, rows, cols], 2, p).start()

        @pl.when(holds)
        def _():
            kvsnd[p] = kvmid[wf[6, p]]

            @pl.when(p != me)
            def _():
                to_dp(kvsnd.at[p], kvfin.at[head], 3, p).start()

        return c

    lax.fori_loop(0, 64, collect, 0)
    own = pltpu.make_async_copy(snd.at[me], fin.at[:, rows, cols], lsem.at[0])
    own.start()

    @pl.when(holds)
    def _():
        c = pltpu.make_async_copy(kvsnd.at[me], kvfin.at[head], lsem.at[1])
        c.start()
        c.wait()
        landed(kvfin.at[pl.ds(0, 15)], rsem.at[3])

    @pl.when(jnp.logical_not(holds))
    def _():
        landed(kvfin, rsem.at[3])

    own.wait()
    landed(mid.at[pl.ds(0, 63)], rsem.at[2])

    landed(x.at[pl.ds(0, 63)], ssem.at[0])
    landed(x.at[pl.ds(0, 63)], ssem.at[2])

    @pl.when(holds)
    def _():
        landed(kvmid.at[pl.ds(0, 15)], ssem.at[1])
        landed(kvmid.at[pl.ds(0, 63)], ssem.at[3])

    @pl.when(jnp.logical_not(holds))
    def _():
        landed(kvmid.at[pl.ds(0, 16)], ssem.at[1])

    for hop in range(1, 5):
        @pl.when(ctx + hop <= 7)
        def _():
            landed(k, gsem.at[hop - 1])
            landed(v, gsem.at[hop + 3])

        @pl.when(ctx - hop >= 0)
        def _():
            landed(red.at[hop - 1, 0], bsem.at[hop - 1])
            landed(red.at[hop - 1, 1], bsem.at[hop + 3])


def place_kernel(fin, kvfin, out_h, dq_h, dk_h, dv_h, sem):
    ends = [
        pltpu.make_async_copy(fin.at[0], out_h, sem.at[0]),
        pltpu.make_async_copy(fin.at[1], dq_h, sem.at[1]),
        pltpu.make_async_copy(kvfin.at[pl.ds(0, 8)], dk_h, sem.at[2]),
        pltpu.make_async_copy(kvfin.at[pl.ds(8, 8)], dv_h, sem.at[3]),
    ]
    for c in ends:
        c.start()
    for c in ends:
        c.wait()


def body(queries, keys, values, grad_out, doc_lengths, switches):
    wide = jax.ShapeDtypeStruct((128, 2048), BF)
    narrow = jax.ShapeDtypeStruct((8, 16, 128), BF)
    vmem = pl.BlockSpec(memory_space=pltpu.VMEM)
    hbm = pl.BlockSpec(memory_space=pltpu.HBM)
    dma = pltpu.SemaphoreType.DMA
    fin, kvfin = pl.pallas_call(
        kernel,
        out_shape=(
            jax.ShapeDtypeStruct((2, 128, 2048), BF),
            jax.ShapeDtypeStruct((16, 16, 128), BF),
        ),
        in_specs=[hbm] * 6,
        out_specs=[vmem, vmem],
        scratch_shapes=[
            pltpu.VMEM((128, 2048), BF),
            pltpu.VMEM((128, 2048), BF),
            pltpu.VMEM((640, 128), BF),
            pltpu.VMEM((640, 128), BF),
            pltpu.VMEM((128, 640), BF),
            pltpu.VMEM((128, 640), BF),
            pltpu.VMEM((640, 256), F32),
            pltpu.VMEM((640, 128), F32),
            pltpu.VMEM((640, 128), F32),
            pltpu.VMEM((4, 2, 128, 128), F32),
            pltpu.VMEM((64, 2, 32, 128), BF),
            pltpu.VMEM((64, 2, 32, 128), BF),
            pltpu.VMEM((64, 2, 32, 128), BF),
            pltpu.VMEM((16, 16, 128), BF),
            pltpu.VMEM((64, 16, 128), BF),
            pltpu.VMEM((64, 16, 128), BF),
            pltpu.SMEM((8, 64), jnp.int32),
            pltpu.SMEM((6, 64), jnp.int32),
            pltpu.SMEM((7, 64), jnp.int32),
            dma((4,)), dma((4,)), dma((2,)), dma((6,)),
            dma((8,)), dma((8,)), dma((8,)), dma((8,)), pltpu.SemaphoreType.REGULAR,
        ],
        compiler_params=pltpu.CompilerParams(
            collective_id=0, has_side_effects=True, vmem_limit_bytes=60 << 20
        ),
        cost_estimate=pl.CostEstimate(
            flops=2_000_000_000, bytes_accessed=4 << 20, transcendentals=1_300_000
        ),
    )(doc_lengths.T, switches, queries[0], keys[0], values[0], grad_out[0])
    out, dq, dk, dv = pl.pallas_call(
        place_kernel,
        out_shape=(wide, wide, narrow, narrow),
        in_specs=[vmem, vmem],
        out_specs=[hbm] * 4,
        scratch_shapes=[dma((4,))],
        cost_estimate=pl.CostEstimate(flops=0, bytes_accessed=2 << 20, transcendentals=0),
    )(fin, kvfin)
    return (out[None], dq[None], dk.reshape(1, 128, 128), dv.reshape(1, 128, 128))


def solution(mesh):
    split = P("dp", "ctx", None)
    return jax.shard_map(
        body,
        mesh=mesh,
        in_specs=(split, split, split, split, P(), P()),
        out_specs=(split, split, split, split),
        check_vma=False,
    )
```

```python
import jax
import jax.numpy as jnp
from jax import lax
from jax.experimental import pallas as pl
from jax.experimental.pallas import tpu as pltpu
from jax.sharding import PartitionSpec as P

NEG_FILL = -1e30
BF = jnp.bfloat16
F32 = jnp.float32
MESH = pl.DeviceIdType.MESH
SCALE = 128 ** (-0.5)
NT = (((1,), (1,)), ((), ()))
NN = (((1,), (0,)), ((), ()))


def dot(a, b, dims):
    return lax.dot_general(a, b, dims, preferred_element_type=F32)


def ring_at(ring, me):
    half = (ring + 1) // 2
    return (me // 4 + 8 + jnp.where(ring % 2 == 1, half, -half)) % 16


def plane_at(ring, me):
    return 8 * (ring // 8) + (ring + me // 4) % 8


def peer_at(step, me):
    return plane_at(step // 4, me) * 4 + (me % 4 + step) % 4


def landed(ref, sem):
    pltpu.make_async_copy(ref, ref, sem).wait()


def kernel(
    lengths_h, switches_h, q_h, k, v, g_h, fin, kvfin,
    q, g, kw, vw, kt, vt, bias, dks, dvs, red, x, mid_out, mid_dq, snd, kvx, kvmid, kvsnd, lengths, switches, wf,
    ssem, rsem, lsem, isem, gsem, hsem, bsem, csem, ready,
):
    me = lax.axis_index("dp")
    ctx = lax.axis_index("ctx")
    head, part = me // 4, me % 4
    holds = part == head % 4
    barrier = pltpu.get_barrier_semaphore()
    fetches = [
        pltpu.make_async_copy(k, kw.at[pl.ds(512, 128)], isem.at[0]),
        pltpu.make_async_copy(v, vw.at[pl.ds(512, 128)], isem.at[1]),
        pltpu.make_async_copy(q_h, q, isem.at[2]),
        pltpu.make_async_copy(g_h, g, isem.at[3]),
        pltpu.make_async_copy(lengths_h, lengths, isem.at[4]),
        pltpu.make_async_copy(switches_h, switches, isem.at[5]),
    ]
    for c in fetches:
        c.start()

    def greet(p):
        pl.semaphore_signal(barrier, inc=1, device_id={"dp": p}, device_id_type=MESH)

    def greet_column(step, c):
        greet((me + 4 * step) % 64)
        return c

    def neighbour(lane):
        return 4 * head + (part + lane) % 4

    lax.fori_loop(1, 16, greet_column, 0)
    for lane in range(1, 4):
        greet(neighbour(lane))
    for hop in range(1, 5):
        @pl.when(ctx + hop <= 7)
        def _():
            pl.semaphore_signal(barrier, inc=1, device_id={"ctx": ctx + hop}, device_id_type=MESH)

        @pl.when(ctx - hop >= 0)
        def _():
            pl.semaphore_signal(barrier, inc=1, device_id={"ctx": ctx - hop}, device_id_type=MESH)

    pl.semaphore_wait(barrier, 18 + jnp.minimum(ctx, 4) + jnp.minimum(7 - ctx, 4))

    def to_ctx(src, dst, send, recv, peer):
        return pltpu.make_async_remote_copy(
            src_ref=src, dst_ref=dst, send_sem=send, recv_sem=recv,
            device_id={"ctx": peer}, device_id_type=MESH,
        )

    def to_dp(src, dst, which, peer):
        return pltpu.make_async_remote_copy(
            src_ref=src, dst_ref=dst, send_sem=ssem.at[which], recv_sem=rsem.at[which],
            device_id={"dp": peer}, device_id_type=MESH,
        )

    for ref, place, base in ((k, kw, 0), (v, vw, 4)):
        for hop in range(1, 5):
            @pl.when(ctx + hop <= 7)
            def _():
                to_ctx(
                    ref, place.at[pl.ds(128 * (4 - hop), 128)], gsem.at[base + hop - 1],
                    hsem.at[base + hop - 1], ctx + hop,
                ).start()

    for lane in range(1, 4):
        pl.semaphore_signal(
            ready, inc=1, device_id={"dp": neighbour(lane)}, device_id_type=MESH
        )

    for c in fetches:
        c.wait()

    row_pos = 128 * ctx + lax.broadcasted_iota(jnp.int32, (1, 256), 1) % 128
    key_pos = 128 * (ctx - 4) + lax.broadcasted_iota(jnp.int32, (640, 256), 0)
    first = jnp.int32(0)
    starts = jnp.zeros((1, 256), jnp.int32)
    for doc in range(8):
        starts = jnp.where(first <= row_pos, jnp.maximum(starts, first), starts)
        first = first + lengths[doc, me]
    bias[...] = jnp.where((key_pos <= row_pos) & (key_pos >= starts), 0.0, NEG_FILL)

    dks[...] = jnp.zeros_like(dks)
    dvs[...] = jnp.zeros_like(dvs)
    for hop in range(1, 5):
        rows = pl.ds(128 * (4 - hop), 128)

        @pl.when(ctx - hop < 0)
        def _():
            kw[rows] = jnp.zeros((128, 128), BF)
            vw[rows] = jnp.zeros((128, 128), BF)

    for hop in range(1, 5):
        @pl.when(ctx - hop >= 0)
        def _():
            landed(k, hsem.at[hop - 1])

    pl.semaphore_wait(ready, 3)

    def pair(i, c):
        ha, hb = ring_at(2 * i, me), ring_at(2 * i + 1, me)
        ca = pl.ds(pl.multiple_of(128 * ha, 128), 128)
        cb = pl.ds(pl.multiple_of(128 * hb, 128), 128)
        q2 = jnp.concatenate([q[:, ca], q[:, cb]], axis=0)
        g2 = jnp.concatenate([g[:, ca], g[:, cb]], axis=0)
        s = dot(kw[...], q2, NT) * SCALE + bias[...]
        e = jnp.exp(s - jnp.max(s, axis=0, keepdims=True))
        w = e * (1.0 / jnp.sum(e, axis=0, keepdims=True))
        rounded = w.astype(BF)

        @pl.when(i == 0)
        def _():
            kt[...] = kw[...].T
            for hop in range(1, 5):
                @pl.when(ctx - hop >= 0)
                def _():
                    landed(v, hsem.at[hop + 3])

            vt[...] = vw[...].T

        ot = dot(vt[...], rounded, NN).astype(BF).astype(F32)
        dots = jnp.sum(ot * g2.astype(F32).T, axis=0, keepdims=True)
        ds = (w * (dot(vw[...], g2, NT) - dots) * SCALE).astype(BF)
        dqt = dot(kt[...], ds, NN)
        dks[...] += dot(ds, q2, NN)
        dvs[...] += dot(rounded, g2, NN)
        o = ot.T.astype(BF).reshape(8, 32, 128)
        dq = dqt.T.astype(BF).reshape(8, 32, 128)
        for n in range(4):
            x[4 * ha + n, 0] = o[n]
            x[4 * ha + n, 1] = dq[n]
            x[4 * hb + n, 0] = o[4 + n]
            x[4 * hb + n, 1] = dq[4 + n]
        for n in range(8):
            p = ring_at((8 * i + n) // 4, me) * 4 + (me % 4 + n) % 4

            @pl.when(p != me)
            def _():
                to_dp(x.at[p, 0], mid_out.at[me], 0, p).start()

        return c

    lax.fori_loop(0, 8, pair, 0)

    def scatter(step, c):
        p = ring_at(step // 4, me) * 4 + (me % 4 + step) % 4

        @pl.when(p != me)
        def _():
            to_dp(x.at[p, 1], mid_dq.at[me], 4, p).start()

        return c

    lax.fori_loop(0, 64, scatter, 0)
    owns = [
        pltpu.make_async_copy(x.at[me, 0], mid_out.at[me], lsem.at[0]),
        pltpu.make_async_copy(x.at[me, 1], mid_dq.at[me], lsem.at[2]),
    ]
    for c in owns:
        c.start()

    for hop in range(1, 5):
        rows = pl.ds(128 * (4 - hop), 128)

        @pl.when(ctx - hop >= 0)
        def _():
            to_ctx(dks.at[rows], red.at[hop - 1, 0], bsem.at[hop - 1], csem.at[hop - 1], ctx - hop).start()
            to_ctx(dvs.at[rows], red.at[hop - 1, 1], bsem.at[hop + 3], csem.at[hop + 3], ctx - hop).start()

        @pl.when(ctx + hop > 7)
        def _():
            red[hop - 1] = jnp.zeros((2, 128, 128), F32)

    def begin(r, c):
        wf[0, r] = r
        return c

    lax.fori_loop(0, 64, begin, 0)
    for bit in range(6):
        def section(r, c):
            size = 1 << bit
            other = r + size * (1 - 2 * ((r // size) % 2))
            wf[bit + 1, r] = jnp.where(switches[bit, r] == 1, wf[bit, other], wf[bit, r])
            return c

        lax.fori_loop(0, 64, section, 0)

    for hop in range(1, 5):
        @pl.when(ctx + hop <= 7)
        def _():
            landed(red.at[hop - 1, 0], csem.at[hop - 1])
            landed(red.at[hop - 1, 1], csem.at[hop + 3])

    total_k = dks[pl.ds(512, 128)] + ((red[0, 0] + red[1, 0]) + (red[2, 0] + red[3, 0]))
    total_v = dvs[pl.ds(512, 128)] + ((red[0, 1] + red[1, 1]) + (red[2, 1] + red[3, 1]))
    kvx[pl.ds(0, 8)] = total_k.astype(BF).reshape(8, 16, 128)
    kvx[pl.ds(8, 8)] = total_v.astype(BF).reshape(8, 16, 128)

    def scatter_kv(i, c):
        t = (head + 8 + i) % 16
        p = 4 * t + t % 4

        @pl.when(p != me)
        def _():
            to_dp(kvx.at[t], kvmid.at[me], 1, p).start()

        return c

    lax.fori_loop(0, 16, scatter_kv, 0)

    for c in owns:
        c.wait()
    most = pl.ds(0, 63)
    rows = pl.ds(pl.multiple_of(32 * part, 32), 32)
    cols = pl.ds(pl.multiple_of(128 * head, 128), 128)

    landed(mid_out.at[most], rsem.at[0])

    def collect_out(step, c):
        p = peer_at(step, me)
        snd[p, 0] = mid_out[wf[6, p]]

        @pl.when(p != me)
        def _():
            to_dp(snd.at[p, 0], fin.at[0, rows, cols], 2, p).start()

        return c

    lax.fori_loop(0, 64, collect_out, 0)

    @pl.when(holds)
    def _():
        c = pltpu.make_async_copy(kvx.at[head], kvmid.at[me], lsem.at[1])
        c.start()
        c.wait()
        landed(kvmid.at[most], rsem.at[1])

    landed(mid_dq.at[most], rsem.at[4])

    def collect(step, c):
        p = peer_at(step, me)
        snd[p, 1] = mid_dq[wf[6, p]]

        @pl.when(p != me)
        def _():
            to_dp(snd.at[p, 1], fin.at[1, rows, cols], 5, p).start()

        @pl.when(holds)
        def _():
            kvsnd[p] = kvmid[wf[6, p]]

            @pl.when(p != me)
            def _():
                to_dp(kvsnd.at[p], kvfin.at[head], 3, p).start()

        return c

    lax.fori_loop(0, 64, collect, 0)
    own = pltpu.make_async_copy(snd.at[me], fin.at[:, rows, cols], lsem.at[0])
    own.start()

    @pl.when(holds)
    def _():
        c = pltpu.make_async_copy(kvsnd.at[me], kvfin.at[head], lsem.at[1])
        c.start()
        c.wait()
        landed(kvfin.at[pl.ds(0, 15)], rsem.at[3])

    @pl.when(jnp.logical_not(holds))
    def _():
        landed(kvfin, rsem.at[3])

    own.wait()
    landed(mid_out.at[most], rsem.at[2])
    landed(mid_dq.at[most], rsem.at[5])

    for t, which in ((0, 0), (1, 4), (0, 2), (1, 5)):
        landed(x.at[most, t], ssem.at[which])

    @pl.when(holds)
    def _():
        landed(kvmid.at[pl.ds(0, 15)], ssem.at[1])
        landed(kvmid.at[pl.ds(0, 63)], ssem.at[3])

    @pl.when(jnp.logical_not(holds))
    def _():
        landed(kvmid.at[pl.ds(0, 16)], ssem.at[1])

    for hop in range(1, 5):
        @pl.when(ctx + hop <= 7)
        def _():
            landed(k, gsem.at[hop - 1])
            landed(v, gsem.at[hop + 3])

        @pl.when(ctx - hop >= 0)
        def _():
            landed(red.at[hop - 1, 0], bsem.at[hop - 1])
            landed(red.at[hop - 1, 1], bsem.at[hop + 3])


def place_kernel(fin, kvfin, out_h, dq_h, dk_h, dv_h, sem):
    ends = [
        pltpu.make_async_copy(fin.at[0], out_h, sem.at[0]),
        pltpu.make_async_copy(fin.at[1], dq_h, sem.at[1]),
        pltpu.make_async_copy(kvfin.at[pl.ds(0, 8)], dk_h, sem.at[2]),
        pltpu.make_async_copy(kvfin.at[pl.ds(8, 8)], dv_h, sem.at[3]),
    ]
    for c in ends:
        c.start()
    for c in ends:
        c.wait()


def body(queries, keys, values, grad_out, doc_lengths, switches):
    wide = jax.ShapeDtypeStruct((128, 2048), BF)
    narrow = jax.ShapeDtypeStruct((8, 16, 128), BF)
    vmem = pl.BlockSpec(memory_space=pltpu.VMEM)
    hbm = pl.BlockSpec(memory_space=pltpu.HBM)
    dma = pltpu.SemaphoreType.DMA
    fin, kvfin = pl.pallas_call(
        kernel,
        out_shape=(
            jax.ShapeDtypeStruct((2, 128, 2048), BF),
            jax.ShapeDtypeStruct((16, 16, 128), BF),
        ),
        in_specs=[hbm] * 6,
        out_specs=[vmem, vmem],
        scratch_shapes=[
            pltpu.VMEM((128, 2048), BF),
            pltpu.VMEM((128, 2048), BF),
            pltpu.VMEM((640, 128), BF),
            pltpu.VMEM((640, 128), BF),
            pltpu.VMEM((128, 640), BF),
            pltpu.VMEM((128, 640), BF),
            pltpu.VMEM((640, 256), F32),
            pltpu.VMEM((640, 128), F32),
            pltpu.VMEM((640, 128), F32),
            pltpu.VMEM((4, 2, 128, 128), F32),
            pltpu.VMEM((64, 2, 32, 128), BF),
            pltpu.VMEM((64, 32, 128), BF),
            pltpu.VMEM((64, 32, 128), BF),
            pltpu.VMEM((64, 2, 32, 128), BF),
            pltpu.VMEM((16, 16, 128), BF),
            pltpu.VMEM((64, 16, 128), BF),
            pltpu.VMEM((64, 16, 128), BF),
            pltpu.SMEM((8, 64), jnp.int32),
            pltpu.SMEM((6, 64), jnp.int32),
            pltpu.SMEM((7, 64), jnp.int32),
            dma((6,)), dma((6,)), dma((3,)), dma((6,)),
            dma((8,)), dma((8,)), dma((8,)), dma((8,)), pltpu.SemaphoreType.REGULAR,
        ],
        compiler_params=pltpu.CompilerParams(
            collective_id=0, has_side_effects=True, vmem_limit_bytes=60 << 20
        ),
        cost_estimate=pl.CostEstimate(
            flops=2_000_000_000, bytes_accessed=4 << 20, transcendentals=1_300_000
        ),
    )(doc_lengths.T, switches, queries[0], keys[0], values[0], grad_out[0])
    out, dq, dk, dv = pl.pallas_call(
        place_kernel,
        out_shape=(wide, wide, narrow, narrow),
        in_specs=[vmem, vmem],
        out_specs=[hbm] * 4,
        scratch_shapes=[dma((4,))],
        cost_estimate=pl.CostEstimate(flops=0, bytes_accessed=2 << 20, transcendentals=0),
    )(fin, kvfin)
    return (out[None], dq[None], dk.reshape(1, 128, 128), dv.reshape(1, 128, 128))


def solution(mesh):
    split = P("dp", "ctx", None)
    return jax.shard_map(
        body,
        mesh=mesh,
        in_specs=(split, split, split, split, P(), P()),
        out_specs=(split, split, split, split),
        check_vma=False,
    )
```
